32 devices in a mesh: dp: 8 (over z, x), zero: 4 (over y, core).
Axes of the slice: x: 2, y: 2, z: 4, core: 2. Of those that a mesh axis runs over, the one named last changes fastest.
Arguments:
- tokens: bfloat16 [16384, 256], P(('dp', 'zero')), may hold values from -6 to 6
- cotangent: bfloat16 [16384, 256], P(('dp', 'zero')), may hold values from -6 to 6
- lengths: int32 [32, 2], P(('dp', 'zero')), may hold values from 0 to 512, as said below
- qkv_weight: float32 [256, 768], P('zero'), may hold values from -0.375 to 0.375
- out_weight: float32 [256, 256], P('zero'), may hold values from -3 to 3
- up_weight: float32 [256, 1024], P('zero'), may hold values from -0.375 to 0.375
- down_weight: float32 [1024, 256], P('zero'), may hold values from -0.1875 to 0.1875
- vectors: float32 [3328], P('zero'), may hold values from -0.8 to 1.4, as said below
- qkv_first: float32 [256, 768], P('zero'), may hold values from -24 to 24
- out_first: float32 [256, 256], P('zero'), may hold values from -24 to 24
- up_first: float32 [256, 1024], P('zero'), may hold values from -24 to 24
- down_first: float32 [1024, 256], P('zero'), may hold values from -24 to 24
- vectors_first: float32 [3328], P('zero'), may hold values from -80 to 80
- qkv_second: float32 [256, 768], P('zero'), may hold values from 32.768 to 491.52
- out_second: float32 [256, 256], P('zero'), may hold values from 32.768 to 491.52
- up_second: float32 [256, 1024], P('zero'), may hold values from 32.768 to 491.52
- down_second: float32 [1024, 256], P('zero'), may hold values from 32.768 to 491.52
- vectors_second: float32 [3328], P('zero'), may hold values from 327.68 to 4915.2
Outputs:
- activations: bfloat16 [16384, 256], P(('dp', 'zero'))
- input_grad: bfloat16 [16384, 256], P(('dp', 'zero'))
- qkv_updated: float32 [256, 768], P('zero')
- out_updated: float32 [256, 256], P('zero')
- up_updated: float32 [256, 1024], P('zero')
- down_updated: float32 [1024, 256], P('zero')
- vectors_updated: float32 [3328], P('zero')
- qkv_momentum: float32 [256, 768], P('zero')
- out_momentum: float32 [256, 256], P('zero')
- up_momentum: float32 [256, 1024], P('zero')
- down_momentum: float32 [1024, 256], P('zero')
- vectors_momentum: float32 [3328], P('zero')
- qkv_variance: float32 [256, 768], P('zero')
- out_variance: float32 [256, 256], P('zero')
- up_variance: float32 [256, 1024], P('zero')
- down_variance: float32 [1024, 256], P('zero')
- vectors_variance: float32 [3328], P('zero')
The draws below stay inside these ranges and needn't reach their ends.
Inputs may be any that keep to these rules, and one draw needn't show every extreme that they name: Row b lists the lengths of the two sequences of buffer b; a row sums to between 256 and 512, its first entry is at least half of its sum, and some buffer holds one sequence of 512 tokens and an empty second one. `vectors`: g1 and g2 lie near one, the biases near zero.
All inputs are finite; a program needn't handle non-finite values.
Results may differ from the reference program's by a relative error of at most 0.0055.
The reference program's roundings to bfloat16 on the way count: a program that leaves them out, or rounds other values in their place, can miss the bound.
Values may be sent and summed in bfloat16 or wider, within the bound.
A program may use at most 64 MiB of HBM per device.

```python
import math
import jax
import jax.numpy as jnp
from jax import lax

D = 256
HEADS = 8
HEAD_DIM = 32
ROT = 8
FF = 1024
TOK_DEV = 512
STEP = 5
BUFFERS = 32
TOKENS = 16384
VEC = 3328


def draw_lengths(key, part):
    key = jax.random.fold_in(key, 5)
    load_key, split_key, full_key = jax.random.split(key, 3)
    totals = TOK_DEV - jax.random.randint(load_key, (BUFFERS,), 0, TOK_DEV // 2 + 1)
    firsts = jax.random.randint(split_key, (BUFFERS,), (totals + 1) // 2, totals + 1)
    chosen = jax.random.randint(full_key, (), 0, BUFFERS)
    picked = jnp.arange(BUFFERS) == chosen
    seconds = jnp.where(picked, 0, totals - firsts)
    firsts = jnp.where(picked, TOK_DEV, firsts)
    return jnp.stack([firsts, seconds], axis=1).astype(jnp.int32)


def draw_vectors(key, part):
    key = jax.random.fold_in(key, 9)
    gain_key, bias_key = jax.random.split(key)
    gains = jax.random.uniform(gain_key, (2 * D,), jnp.float32, 0.6, 1.4)
    biases = jnp.clip(0.2 * jax.random.normal(bias_key, (7 * D + FF,), jnp.float32), -0.8, 0.8)
    return jnp.concatenate([gains[:D], biases[:D], gains[D:], biases[D:2 * D], biases[2 * D:]])


def block_levels(own_key, shape, cuts, least, largest):
    factor_of, own = 1.0, jax.random.fold_in(own_key, 6)
    for dim, shards_of in cuts:
        heights = jnp.exp(jax.random.uniform(jax.random.fold_in(own, dim), (shards_of,), jnp.float32, least / len(cuts), largest / len(cuts)))
        factor_of = factor_of * jnp.repeat(heights, shape[dim] // shards_of).reshape([-1 if axis == dim else 1 for axis in range(len(shape))])
    return factor_of


def scatter_about(stream_key, shape, scale, reach, cuts=(), kind=jnp.bfloat16):
    values = jax.random.normal(stream_key, shape, jnp.float32) * scale
    if len(cuts) > 0:
        values = block_levels(stream_key, shape, cuts, -0.22, 0.18) * values
    return jnp.clip(values, min=-reach, max=reach).astype(kind)


def setup_inputs(seed: int = 0) -> dict:
    key_of = jax.random.split(jax.random.key(seed), 19)
    return {
        "tokens": scatter_about(key_of[0], (TOKENS, D), 1.0, 6.0, ((0, 32),)),
        "cotangent": scatter_about(key_of[1], (TOKENS, D), 1.0, 6.0, ((0, 32),)),
        "lengths": draw_lengths(jax.random.fold_in(key_of[18], 71), 0),
        "qkv_weight": scatter_about(key_of[3], (D, 3 * D), D ** -0.5, 0.375, ((0, 4),), jnp.float32),
        "out_weight": scatter_about(key_of[4], (D, D), (D // 64) ** -0.5, 3.0, ((0, 4),), jnp.float32),
        "up_weight": scatter_about(key_of[5], (D, FF), D ** -0.5, 0.375, ((0, 4),), jnp.float32),
        "down_weight": scatter_about(key_of[6], (FF, D), FF ** -0.5, 0.1875, ((0, 4),), jnp.float32),
        "vectors": draw_vectors(jax.random.fold_in(key_of[18], 71), 0),
        "qkv_first": scatter_about(key_of[8], (D, 3 * D), (0.03 * TOKENS ** 0.5), 24.0, ((0, 4),), jnp.float32),
        "out_first": scatter_about(key_of[9], (D, D), (0.03 * TOKENS ** 0.5), 24.0, ((0, 4),), jnp.float32),
        "up_first": scatter_about(key_of[10], (D, FF), (0.03 * TOKENS ** 0.5), 24.0, ((0, 4),), jnp.float32),
        "down_first": scatter_about(key_of[11], (FF, D), (0.03 * TOKENS ** 0.5), 24.0, ((0, 4),), jnp.float32),
        "vectors_first": scatter_about(key_of[12], (VEC,), (0.1 * TOKENS ** 0.5), 80.0, ((0, 4),), jnp.float32),
        "qkv_second": jnp.clip(jnp.exp(math.log(491.52) - 2.70805 * jax.random.uniform(key_of[13], (D, 3 * D), jnp.float32) ** block_levels(key_of[13], (D, 3 * D), ((0, 4),), -0.2, 0.2)), 32.768, 491.52),
        "out_second": jnp.clip(jnp.exp(math.log(491.52) - 2.70805 * jax.random.uniform(key_of[14], (D, D), jnp.float32) ** block_levels(key_of[14], (D, D), ((0, 4),), -0.2, 0.2)), 32.768, 491.52),
        "up_second": jnp.clip(jnp.exp(math.log(491.52) - 2.70805 * jax.random.uniform(key_of[15], (D, FF), jnp.float32) ** block_levels(key_of[15], (D, FF), ((0, 4),), -0.2, 0.2)), 32.768, 491.52),
        "down_second": jnp.clip(jnp.exp(math.log(491.52) - 2.70805 * jax.random.uniform(key_of[16], (FF, D), jnp.float32) ** block_levels(key_of[16], (FF, D), ((0, 4),), -0.2, 0.2)), 32.768, 491.52),
        "vectors_second": jnp.clip(jnp.exp(math.log(4915.2) - 2.7080503 * jax.random.uniform(key_of[17], (VEC,), jnp.float32) ** block_levels(key_of[17], (VEC,), ((0, 4),), -0.2, 0.2)), 327.68, 4915.2),
    }


NORM_EPS = 1e-05
BETA_ONE = 0.9
BETA_TWO = 0.95
ADAM_EPS = 1e-08
DECAY = 0.01
RATE_MATRIX = 0.06
RATE_OUTPUT = 0.3
RATE_VECTOR = 0.5
NEGATIVE = -1e+30
HIGH = lax.Precision.HIGHEST

@jax.custom_vjp
def low(v):
    return lax.optimization_barrier(v.astype(jnp.bfloat16)).astype(jnp.float32)

@jax.custom_vjp
def low_back(v):
    return v

def low_keep(v):
    return (low(v), None)

def low_pass(kept, grad):
    return (grad,)

def back_keep(v):
    return (v, None)

def back_low(kept, grad):
    return (low(grad),)
low.defvjp(low_keep, low_pass)
low_back.defvjp(back_keep, back_low)

def layout(pair, count):
    first = pair[0]
    total = pair[0] + pair[1]
    index = jnp.arange(count, dtype=jnp.int32)
    segment = (index >= first).astype(jnp.int32) + (index >= total).astype(jnp.int32)
    start = jnp.where(segment == 0, 0, jnp.where(segment == 1, first, total))
    position = (index - start).astype(jnp.float32)
    live = (index < total).astype(jnp.float32)
    return (segment, position, live)

def unpack(vector, width, hidden):
    sizes_list = (width, width, width, width, 3 * width, width, hidden, width)
    pieces = []
    begin = 0
    for length in sizes_list:
        pieces.append(vector[begin:begin + length])
        begin = begin + length
    return pieces

def normalize(rows):
    centered = rows - lax.optimization_barrier(jnp.mean(rows, axis=1, keepdims=True))
    return centered * lax.rsqrt(lax.optimization_barrier(jnp.mean(centered * centered, axis=1, keepdims=True)) + NORM_EPS)

def both_norms(rows, gain_one, bias_one, gain_two, bias_two):
    plain = normalize(rows)
    return (plain * gain_one + bias_one, plain * gain_two + bias_two)

def rotate(lines, position, sign):
    count = lines.shape[0]
    half = ROT // 2
    shaped = lines.reshape(count, -1, HEAD_DIM)
    freq = 1.0 / 10000.0 ** (jnp.arange(half, dtype=jnp.float32) * 2.0 / ROT)
    angle = position[:, None] * freq[None, :]
    cosine = jnp.cos(angle)[:, None, :]
    sine = sign * jnp.sin(angle)[:, None, :]
    lower = shaped[:, :, :half]
    upper = shaped[:, :, half:ROT]
    turned = jnp.concatenate([lower * cosine - upper * sine, upper * cosine + lower * sine, shaped[:, :, ROT:]], axis=2)
    return turned.reshape(count, -1)

def attend(query, keys, values, segment):
    count = query.shape[0]
    block = min(512, count)
    scale = HEAD_DIM ** (-0.5)
    key_heads = keys.reshape(count, HEADS, HEAD_DIM)
    value_heads = values.reshape(count, HEADS, HEAD_DIM)
    key_index = jnp.arange(count, dtype=jnp.int32)

    def one_block(number):
        begin = (number * block).astype(jnp.int32)
        rows = lax.dynamic_slice_in_dim(query, begin, block, 0).reshape(block, HEADS, HEAD_DIM)
        row_index = begin + jnp.arange(block, dtype=jnp.int32)
        row_segment = lax.dynamic_slice_in_dim(segment, begin, block, 0)
        allowed = (row_segment[:, None] == segment[None, :]) & (key_index[None, :] <= row_index[:, None])
        scores = low_back(jnp.einsum('qhd,khd->hqk', rows, key_heads, precision=HIGH) * scale)
        scores = jnp.where(allowed[None], scores, NEGATIVE)
        raised = jnp.exp(scores - lax.optimization_barrier(jnp.max(scores, axis=2, keepdims=True)))
        weights = low(raised / lax.optimization_barrier(jnp.sum(raised, axis=2, keepdims=True)))
        return jnp.einsum('hqk,khd->qhd', weights, value_heads, precision=HIGH).reshape(block, -1)
    mixed = lax.map(jax.checkpoint(one_block), jnp.arange(count // block, dtype=jnp.int32))
    return mixed.reshape(count, -1)

def forward(rows, qkv_w, out_w, up_w, down_w, vector, segment, position, live):
    gain_one, bias_one, gain_two, bias_two, qkv_bias, out_bias, up_bias, down_bias = unpack(vector, D, FF)
    norm_one, norm_two = both_norms(rows, gain_one, bias_one, gain_two, bias_two)
    hidden_one = low(norm_one)
    hidden_two = low(norm_two)
    lines = low_back(jnp.dot(hidden_one, qkv_w, precision=HIGH, preferred_element_type=jnp.float32) + qkv_bias)
    turned = rotate(lines[:, :2 * D], position, 1.0)
    query = low(turned[:, :D])
    keys = low(turned[:, D:])
    values = low(lines[:, 2 * D:])
    mixed = low_back(low(attend(query, keys, values, segment)))
    attn_out = low_back(jnp.dot(mixed, out_w, precision=HIGH, preferred_element_type=jnp.float32) + out_bias)
    up_lines = low_back(jnp.dot(hidden_two, up_w, precision=HIGH, preferred_element_type=jnp.float32) + up_bias)
    active = low(jax.nn.gelu(up_lines, approximate=False))
    mlp_out = low_back(jnp.dot(active, down_w, precision=HIGH, preferred_element_type=jnp.float32) + down_bias)
    return live[:, None] * (rows + attn_out + mlp_out)

def adamw(master, first, second, grad, rate):
    momentum = BETA_ONE * first + (1.0 - BETA_ONE) * grad
    variance = BETA_TWO * second + (1.0 - BETA_TWO) * grad * grad
    direction = momentum / (1.0 - BETA_ONE ** STEP) / (jnp.sqrt(variance / (1.0 - BETA_TWO ** STEP)) + ADAM_EPS)
    return (master - rate * (direction + DECAY * master), momentum, variance)

def reference(tokens, cotangent, lengths, qkv_weight, out_weight, up_weight, down_weight, vectors, qkv_first, out_first, up_first, down_first, vectors_first, qkv_second, out_second, up_second, down_second, vectors_second):
    working = (low(qkv_weight), low(out_weight), low(up_weight), low(down_weight), low(vectors))
    rows_all = tokens.astype(jnp.float32).reshape(BUFFERS, TOK_DEV, D)
    back_all = cotangent.astype(jnp.float32).reshape(BUFFERS, TOK_DEV, D)

    def one_buffer(carry, item):
        rows, back, pair = item
        segment, position, live = layout(pair, TOK_DEV)

        def run(rows_in, qkv_w, out_w, up_w, down_w, vector):
            return forward(rows_in, qkv_w, out_w, up_w, down_w, vector, segment, position, live)
        result, pull = jax.vjp(run, rows, working[0], working[1], working[2], working[3], working[4])
        grads = pull(back)
        summed = (carry[0] + grads[1], carry[1] + grads[2], carry[2] + grads[3], carry[3] + grads[4], carry[4] + grads[5])
        return (summed, (result.astype(jnp.bfloat16), grads[0].astype(jnp.bfloat16)))
    zeros = tuple((jnp.zeros_like(item) for item in working))
    totals, (outputs, input_grads) = lax.scan(one_buffer, zeros, (rows_all, back_all, lengths))
    qkv_new = adamw(qkv_weight, qkv_first, qkv_second, totals[0], RATE_MATRIX)
    out_new = adamw(out_weight, out_first, out_second, totals[1], RATE_OUTPUT)
    up_new = adamw(up_weight, up_first, up_second, totals[2], RATE_MATRIX)
    down_new = adamw(down_weight, down_first, down_second, totals[3], RATE_MATRIX)
    vec_new = adamw(vectors, vectors_first, vectors_second, totals[4], RATE_VECTOR)
    return (outputs.reshape(TOKENS, D), input_grads.reshape(TOKENS, D), qkv_new[0], out_new[0], up_new[0], down_new[0], vec_new[0], qkv_new[1], out_new[1], up_new[1], down_new[1], vec_new[1], qkv_new[2], out_new[2], up_new[2], down_new[2], vec_new[2])
```

```python
import functools
import math

import jax
import jax.numpy as jnp
from jax import lax
from jax.experimental import pallas as pl
from jax.experimental.pallas import tpu as pltpu
from jax.sharding import PartitionSpec as P

HEADS = 8
HEAD_DIM = 32
ROT = 8
STEP = 5


NORM_EPS = 1e-05
BETA_ONE = 0.9
BETA_TWO = 0.95
ADAM_EPS = 1e-08
DECAY = 0.01
RATE_MATRIX = 0.06
RATE_OUTPUT = 0.3
RATE_VECTOR = 0.5
NEGATIVE = -1e30
MESH = pl.DeviceIdType.MESH
F32 = jnp.float32
BF16 = jnp.bfloat16
VROWS = 32
W = 256


def adamw(master, first, second, grad, rate):
    momentum = BETA_ONE * first + (1.0 - BETA_ONE) * grad
    variance = BETA_TWO * second + (1.0 - BETA_TWO) * grad * grad
    direction = (
        momentum / (1.0 - BETA_ONE**STEP) / (jnp.sqrt(variance / (1.0 - BETA_TWO**STEP)) + ADAM_EPS)
    )
    return (master - rate * (direction + DECAY * master), momentum, variance)


def nn(a, b):
    return lax.dot_general(a, b, (((1,), (0,)), ((), ())), preferred_element_type=F32)


def nt(a, b):
    return lax.dot_general(a, b, (((1,), (1,)), ((), ())), preferred_element_type=F32)


def tn(a, b):
    return lax.dot_general(a, b, (((0,), (0,)), ((), ())), preferred_element_type=F32)


def remote(src, dst, send, recv, device):
    return pltpu.make_async_remote_copy(
        src_ref=src, dst_ref=dst, send_sem=send, recv_sem=recv, device_id=device, device_id_type=MESH
    )


class Reduction:
    def __init__(self, place, full, core_in, y_out, y_in, share, share_low, pieces, total, sems):
        self.place = place
        self.full, self.core_in, self.y_out, self.y_in = full, core_in, y_out, y_in
        self.share, self.share_low, self.pieces, self.total = share, share_low, pieces, total
        self.zs, self.zr, self.ds, self.dr, self.gs, self.gr = sems
        self.piece = pieces.shape[1]
        self.rows = full.shape[2]

    def core_copy(self, slot):
        p = self.place
        y = p.y if slot else 1 - p.y
        return remote(
            self.full.at[1 - p.c, y], self.core_in.at[y], self.zs.at[slot], self.zr.at[slot], {"zero": p.core}
        )

    def y_copy(self):
        return remote(self.y_out, self.y_in, self.zs.at[2], self.zr.at[2], {"zero": self.place.other})

    def rows_of(self, index):
        return pl.ds(pl.multiple_of(index * self.piece, self.piece), self.piece)

    def scatter_copy(self, k):
        p = self.place
        peer = lax.rem(p.dp + k, p.n)
        return remote(
            self.share_low.at[self.rows_of(peer)], self.pieces.at[k], self.ds.at[k], self.dr.at[k], {"dp": peer}
        )

    def gather_copy(self, k):
        p = self.place
        peer = lax.rem(p.dp + k, p.n)
        mine = self.total.at[self.rows_of(p.dp)]
        return remote(mine, mine, self.gs.at[k], self.gr.at[k], {"dp": peer})

    def gather_arrival(self, k):
        p = self.place
        peer = lax.rem(p.dp + p.n - k, p.n)
        theirs = self.total.at[self.rows_of(peer)]
        return remote(theirs, theirs, self.gs.at[k], self.gr.at[k], {"dp": peer})

    def loop(self, action):
        def body(k, carry):
            action(k)
            return carry

        lax.fori_loop(1, self.place.n, body, 0)

    def stage_core(self):
        self.core_copy(0).start()
        self.core_copy(1).start()

    def stage_y(self):
        p = self.place
        self.core_copy(0).wait_recv()
        self.y_out[...] = (self.full[p.c, 1 - p.y] + self.core_in[1 - p.y]).astype(BF16)
        self.y_copy().start()

    def stage_scatter(self):
        p = self.place
        self.core_copy(1).wait_recv()
        self.y_copy().wait_recv()
        summed = self.full[p.c, p.y] + self.core_in[p.y] + self.y_in[...].astype(F32)
        self.share[pl.ds(0, self.rows)] = summed
        self.share_low[pl.ds(0, self.rows)] = summed.astype(BF16)
        spare = self.share.shape[0] - self.rows
        if spare:
            self.share[pl.ds(self.rows, spare)] = jnp.zeros((spare, W), F32)
            self.share_low[pl.ds(self.rows, spare)] = jnp.zeros((spare, W), BF16)
        self.loop(lambda k: self.scatter_copy(k).start())

    def stage_gather(self):
        p = self.place
        self.loop(lambda k: self.scatter_copy(k).wait_recv())
        summed = self.share[self.rows_of(p.dp)]
        if p.n <= 16:
            for k in range(1, p.n):
                summed = summed + self.pieces[k].astype(F32)
        else:
            summed = lax.fori_loop(1, p.n, lambda k, s: s + self.pieces[k].astype(F32), summed)
        self.total[self.rows_of(p.dp)] = summed.astype(self.total.dtype)
        self.loop(lambda k: self.gather_copy(k).start())

    def stage_end(self):
        self.loop(lambda k: self.gather_arrival(k).wait_recv())

    def drain(self):
        self.core_copy(0).wait_send()
        self.core_copy(1).wait_send()
        self.y_copy().wait_send()
        self.loop(lambda k: self.scatter_copy(k).wait_send())
        self.loop(lambda k: self.gather_copy(k).wait_send())


class Place:
    def __init__(self, n):
        self.n = n
        self.dp = lax.axis_index("dp")
        self.z = lax.axis_index("zero")
        self.c = lax.rem(self.z, 2)
        self.y = self.z // 2
        self.core = 2 * self.y + 1 - self.c
        self.other = 2 * (1 - self.y) + self.c
        self.far = 2 * (1 - self.y) + 1 - self.c


def layer_kernel(
    n,
    lengths, tokens, cotangent, qkv_s, out_s, up_s, down_s, vec_s,
    act_o, ig_o, ga_o, gc_o, vec_o,
    qkv_w, out_w, up_w, down_w, vec_in, vec_g, vec_z, vec_t, vec_d,
    gat_s, gat_r, vs, vr, vds, vdr,
    bias_m, q_t, k_t, v_t, do_t, o_t, dlin_t, base, dh2_s,
    a_full, a_core, a_yo, a_yi, a_sh, a_shl, a_pc, a_tot, a_zs, a_zr, a_ds, a_dr, a_gs, a_gr,
    c_full, c_core, c_yo, c_yi, c_sh, c_shl, c_pc, c_tot, c_zs, c_zr, c_ds, c_dr, c_gs, c_gr,
):
    p = Place(n)
    count = tokens.shape[0]
    peers_zero = (p.core, p.other, p.far)
    group_a = Reduction(p, a_full, a_core, a_yo, a_yi, a_sh, a_shl, a_pc, a_tot, (a_zs, a_zr, a_ds, a_dr, a_gs, a_gr))
    group_c = Reduction(p, c_full, c_core, c_yo, c_yi, c_sh, c_shl, c_pc, c_tot, (c_zs, c_zr, c_ds, c_dr, c_gs, c_gr))

    barrier = pltpu.get_barrier_semaphore()
    for peer in peers_zero:
        pl.semaphore_signal(barrier, inc=1, device_id={"zero": peer}, device_id_type=MESH)

    def greet(k, carry):
        peer = lax.rem(p.dp + k, n)
        pl.semaphore_signal(barrier, inc=1, device_id={"dp": peer}, device_id_type=MESH)
        return carry

    lax.fori_loop(1, n, greet, 0)

    weights = (qkv_w, out_w, up_w, down_w)
    for buffer, shard in zip(weights, (qkv_s, out_s, up_s, down_s)):
        buffer[p.z] = shard[...].astype(BF16)
    pl.semaphore_wait(barrier, 3 + n - 1)

    def vec_copy(i, src, dst):
        return remote(src, dst.at[i], vs.at[i], vr.at[i], {"zero": peers_zero[i]})

    def weight_copy(w, way):
        buffer = weights[w]
        shard = p.other if way == 2 else p.z
        device = p.other if way == 1 else p.core
        return remote(buffer.at[shard], buffer.at[shard], gat_s.at[w, way], gat_r.at[w, way], {"zero": device})

    def weight_arrival(w, way):
        buffer = weights[w]
        shard = (p.core, p.other, p.far)[way]
        device = p.other if way == 1 else p.core
        return remote(buffer.at[shard], buffer.at[shard], gat_s.at[w, way], gat_r.at[w, way], {"zero": device})

    for i in range(3):
        vec_copy(i, vec_s, vec_in).start()
    for w in range(4):
        weight_copy(w, 1).start()
        weight_copy(w, 0).start()

    first = lengths[0, 0]
    total = lengths[0, 0] + lengths[0, 1]
    index = lax.broadcasted_iota(jnp.int32, (1, count), 1)
    start = jnp.where(index >= total, total, jnp.where(index >= first, first, 0))
    live = jnp.where(index < total, 1.0, 0.0).astype(F32)
    key_index = lax.broadcasted_iota(jnp.int32, (count, count), 0)
    query_index = lax.broadcasted_iota(jnp.int32, (count, count), 1)
    bias_m[...] = jnp.where((key_index <= query_index) & (key_index >= start), 0.0, NEGATIVE).astype(F32)
    half = ROT // 2
    row = lax.broadcasted_iota(jnp.int32, (ROT, count), 0)
    turn = lax.rem(row, half)
    freq = jnp.where(turn == 0, 1.0, jnp.where(turn == 1, 0.1, jnp.where(turn == 2, 0.01, 0.001))).astype(F32)
    angle = (index - start).astype(F32) * freq
    cosine = jnp.cos(angle)
    sine = jnp.sin(angle) * jnp.where(row < half, -1.0, 1.0).astype(F32)

    def rotate(lines, signed):
        top = lines[:ROT]
        swapped = jnp.concatenate([top[half:], top[:half]], axis=0)
        return jnp.concatenate([top * cosine + swapped * signed, lines[ROT:]], axis=0)

    x = tokens[...].astype(F32).T
    g = (cotangent[...].astype(F32).T * live).astype(BF16)
    centered = x - jnp.mean(x, axis=0, keepdims=True)
    rstd = lax.rsqrt(jnp.mean(centered * centered, axis=0, keepdims=True) + NORM_EPS)
    plain = centered * rstd

    for i in range(3):
        vec_copy(i, vec_s, vec_in).wait_recv()
    vec = (vec_s[...] + vec_in[0] + vec_in[1] + vec_in[2]).astype(BF16).astype(F32).T

    def column(begin, length):
        parts = [vec[:, i : i + 1] for i in range(begin // 128, (begin + length) // 128)]
        return jnp.concatenate(parts, axis=0)

    gain_one, bias_one, gain_two, bias_two = (column(W * i, W) for i in range(4))
    h1 = (plain * gain_one + bias_one).astype(BF16)
    h2 = (plain * gain_two + bias_two).astype(BF16)

    def finish_weight(w):
        weight_arrival(w, 0).wait_recv()
        weight_arrival(w, 2).wait_recv()

    weight_arrival(0, 1).wait_recv()
    weight_copy(0, 2).start()
    weight_arrival(1, 1).wait_recv()
    weight_copy(1, 2).start()
    finish_weight(0)

    scale = HEAD_DIM**-0.5
    for part, target in enumerate((q_t, k_t, v_t)):
        block = qkv_w[:, :, W * part : W * part + W].reshape(W, W)
        lines = tn(block, h1) + column(4 * W + W * part, W)
        for h in range(HEADS):
            piece = lines[HEAD_DIM * h : HEAD_DIM * h + HEAD_DIM]
            if part < 2:
                piece = rotate(piece, sine)
            target[HEAD_DIM * h : HEAD_DIM * h + HEAD_DIM] = piece.astype(BF16)
    finish_weight(1)
    do_t[...] = nn(out_w[...].reshape(W, W), g).astype(BF16)

    weight_arrival(2, 1).wait_recv()
    weight_copy(2, 2).start()

    fold = scale * math.log2(math.e)
    block = count // 2

    def head(h, carry):
        at = pl.ds(pl.multiple_of(h * HEAD_DIM, HEAD_DIM), HEAD_DIM)
        q, k, v, do = q_t[at], k_t[at], v_t[at], do_t[at]
        outs, dqs, dks, dvs = [], [], [], []
        for j in range(2):
            keys = block * (j + 1)
            cut = slice(block * j, block * (j + 1))
            kk, vv, qj, dj = k[:, :keys], v[:, :keys], q[:, cut], do[:, cut]
            scores = tn(kk, qj) * fold + bias_m[:keys, cut]
            raised = jnp.exp2(scores - jnp.max(scores, axis=0, keepdims=True))
            chances = raised * (1.0 / jnp.sum(raised, axis=0, keepdims=True))
            low = chances.astype(BF16)
            outs.append(nn(vv, low))
            inner = tn(vv, dj)
            slope = (chances * (inner - jnp.sum(inner * chances, axis=0, keepdims=True))).astype(BF16)
            dqs.append(nn(kk, slope))
            dks.append(nt(qj, slope))
            dvs.append(nt(dj, low))
        o_t[at] = jnp.concatenate(outs, axis=1).astype(BF16)
        dq = jnp.concatenate(dqs, axis=1) * scale
        dk = jnp.concatenate([dks[0] + dks[1][:, :block], dks[1][:, block:]], axis=1) * scale
        dv = jnp.concatenate([dvs[0] + dvs[1][:, :block], dvs[1][:, block:]], axis=1)
        dlin_t[0, at] = rotate(dq, -sine).astype(BF16)
        dlin_t[1, at] = rotate(dk, -sine).astype(BF16)
        dlin_t[2, at] = dv.astype(BF16)
        return carry

    lax.fori_loop(0, 2, head, 0)
    weight_arrival(3, 1).wait_recv()
    weight_copy(3, 2).start()
    finish_weight(2)
    finish_weight(3)

    ones = jnp.ones((8, count), BF16)

    def put_sum(at, values):
        sums = nt(ones, values)
        for i in range(values.shape[0] // 128):
            vec_g[at // 128 + i : at // 128 + i + 1] = sums[0:1, 128 * i : 128 * i + 128]

    def put_sum_wide(at, values):
        high = values.astype(BF16)
        rest = (values - high.astype(F32)).astype(BF16)
        sums = nt(ones, high) + nt(ones, rest)
        for i in range(values.shape[0] // 128):
            vec_g[at // 128 + i : at // 128 + i + 1] = sums[0:1, 128 * i : 128 * i + 128]

    shard_rows = W // 4
    mlp = jnp.zeros((W, count), F32)
    dh2 = jnp.zeros((W, count), F32)
    for j in range(4):
        w_up = up_w[:, :, W * j : W * j + W].reshape(W, W)
        w_down = down_w[j]
        up = tn(w_up, h2) + column(8 * W + W * j, W)
        phi_sum = 0.5 + 0.5 * lax.erf(up * (0.5**0.5))
        z = (up * phi_sum).astype(BF16)
        bell = jnp.exp2(up * up * (-0.5 * math.log2(math.e))) * ((2.0 * math.pi) ** -0.5)
        du = (nn(w_down, g) * (phi_sum + up * bell)).astype(BF16)
        mlp = mlp + tn(w_down, z)
        dh2 = dh2 + nn(w_up, du)
        a_full[j % 2, j // 2, pl.ds(0, W)] = nt(z, g)
        g_up = nt(h2, du)
        for s in range(4):
            a_full[s % 2, s // 2, pl.ds(W + shard_rows * j, shard_rows)] = g_up[shard_rows * s : shard_rows * (s + 1)]
        put_sum(8 * W + W * j, du)
    group_a.stage_core()
    base[...] = x + mlp + column(12 * W, W)
    dh2_s[...] = dh2

    lax.fori_loop(2, 4, head, 0)
    group_a.stage_y()
    lax.fori_loop(4, 6, head, 0)
    group_a.stage_scatter()
    lax.fori_loop(6, 8, head, 0)

    for j in range(3):
        dlin = dlin_t[j]
        g_qkv = nt(h1, dlin)
        for s in range(4):
            c_full[s % 2, s // 2, pl.ds(shard_rows * j, shard_rows)] = g_qkv[shard_rows * s : shard_rows * (s + 1)]
        put_sum(4 * W + W * j, dlin)
    g_out = nt(o_t[...], g)
    for s in range(4):
        c_full[s % 2, s // 2, pl.ds(3 * shard_rows, shard_rows)] = g_out[shard_rows * s : shard_rows * (s + 1)]
    group_c.stage_core()
    group_a.stage_gather()

    dh1 = jnp.zeros((W, count), F32)
    for j in range(3):
        dh1 = dh1 + nn(qkv_w[:, :, W * j : W * j + W].reshape(W, W), dlin_t[j])
    group_c.stage_y()
    dh2 = dh2_s[...]
    put_sum_wide(0, dh1 * plain)
    put_sum_wide(W, dh1)
    put_sum_wide(2 * W, dh2 * plain)
    put_sum_wide(3 * W, dh2)
    put_sum(7 * W, g)
    put_sum(12 * W, g)
    vec_g[13 * W // 128 : VROWS] = jnp.zeros((VROWS - 13 * W // 128, 128), F32)

    def vec_zero(i):
        return remote(vec_g, vec_z.at[i], vs.at[3 + i], vr.at[3 + i], {"zero": peers_zero[i]})

    for i in range(3):
        vec_zero(i).start()
    group_c.stage_scatter()
    dn = dh1 * gain_one + dh2 * gain_two
    term = (
        dn - jnp.mean(dn, axis=0, keepdims=True) - plain * jnp.mean(dn * plain, axis=0, keepdims=True)
    ) * rstd
    for i in range(3):
        vec_zero(i).wait_recv()
    vec_t[...] = vec_g[...] + vec_z[0] + vec_z[1] + vec_z[2]

    def vec_dp(k):
        peer = lax.rem(p.dp + k, n)
        return remote(vec_t, vec_d.at[k], vds.at[k], vdr.at[k], {"dp": peer})

    group_c.loop(lambda k: vec_dp(k).start())
    ig_o[...] = (g.astype(F32) + term).T.astype(BF16)
    attn = tn(out_w[...].reshape(W, W), o_t[...]) + column(7 * W, W)
    act_o[...] = ((base[...] + attn) * live).T.astype(BF16)

    group_c.stage_gather()
    group_a.stage_end()
    ga_o[...] = a_tot[...].astype(F32)
    group_c.loop(lambda k: vec_dp(k).wait_recv())
    vec_o[...] = lax.fori_loop(1, n, lambda k, s: s + vec_d[k], vec_t[...])
    for w in range(4):
        for way in range(3):
            weight_copy(w, way).wait_send()
    for i in range(3):
        vec_copy(i, vec_s, vec_in).wait_send()
        vec_zero(i).wait_send()
    group_c.loop(lambda k: vec_dp(k).wait_send())
    group_a.drain()
    group_c.stage_end()
    gc_o[...] = c_tot[...].astype(F32)
    group_c.drain()


def piece_rows(rows, n):
    return -(-rows // (16 * n)) * 16


def reduction_scratch(rows, n, kind):
    piece = piece_rows(rows, n)
    dma = pltpu.SemaphoreType.DMA
    return [
        pltpu.VMEM((2, 2, rows, W), F32),
        pltpu.VMEM((2, rows, W), F32),
        pltpu.VMEM((rows, W), BF16),
        pltpu.VMEM((rows, W), BF16),
        pltpu.VMEM((n * piece, W), F32),
        pltpu.VMEM((n * piece, W), BF16),
        pltpu.VMEM((n, piece, W), BF16),
        pltpu.VMEM((n * piece, W), kind),
        dma((3,)), dma((3,)), dma((n,)), dma((n,)), dma((n,)), dma((n,)),
    ]


def layer(n, lengths, tokens, cotangent, qkv, out, up, down, vec):
    count = tokens.shape[0]
    dma = pltpu.SemaphoreType.DMA
    a_rows = n * piece_rows(512, n)
    c_rows = n * piece_rows(256, n)
    vmem = pl.BlockSpec(memory_space=pltpu.VMEM)
    return pl.pallas_call(
        functools.partial(layer_kernel, n),
        out_shape=(
            jax.ShapeDtypeStruct(tokens.shape, BF16),
            jax.ShapeDtypeStruct(tokens.shape, BF16),
            jax.ShapeDtypeStruct((a_rows, W), F32),
            jax.ShapeDtypeStruct((c_rows, W), F32),
            jax.ShapeDtypeStruct((VROWS, 128), F32),
        ),
        in_specs=[pl.BlockSpec(memory_space=pltpu.SMEM)] + [vmem] * 7,
        out_specs=[vmem] * 5,
        scratch_shapes=[
            pltpu.VMEM((4, 64, 3 * W), BF16),
            pltpu.VMEM((4, 64, W), BF16),
            pltpu.VMEM((4, 64, 4 * W), BF16),
            pltpu.VMEM((4, W, W), BF16),
            pltpu.VMEM((3, VROWS, 128), F32),
            pltpu.VMEM((VROWS, 128), F32),
            pltpu.VMEM((3, VROWS, 128), F32),
            pltpu.VMEM((VROWS, 128), F32),
            pltpu.VMEM((n, VROWS, 128), F32),
            dma((4, 3)), dma((4, 3)), dma((6,)), dma((6,)), dma((n,)), dma((n,)),
            pltpu.VMEM((count, count), F32),
            pltpu.VMEM((W, count), BF16),
            pltpu.VMEM((W, count), BF16),
            pltpu.VMEM((W, count), BF16),
            pltpu.VMEM((W, count), BF16),
            pltpu.VMEM((W, count), BF16),
            pltpu.VMEM((3, W, count), BF16),
            pltpu.VMEM((W, count), F32),
            pltpu.VMEM((W, count), F32),
        ]
        + reduction_scratch(512, n, F32)
        + reduction_scratch(256, n, F32),
        compiler_params=pltpu.CompilerParams(
            collective_id=0, has_side_effects=True, vmem_limit_bytes=56 * 1024 * 1024
        ),
        name="layer",
    )(lengths, tokens, cotangent, qkv, out, up, down, vec)


def on_device(
    n,
    tokens,
    cotangent,
    lengths,
    qkv_weight,
    out_weight,
    up_weight,
    down_weight,
    vectors,
    qkv_first,
    out_first,
    up_first,
    down_first,
    vectors_first,
    qkv_second,
    out_second,
    up_second,
    down_second,
    vectors_second,
):
    share = vectors.shape[0]
    begin = lax.axis_index("zero") * share
    vec = lax.dynamic_update_slice(jnp.zeros((VROWS * 128,), F32), vectors, (begin,)).reshape(VROWS, 128)
    activations, input_grad, sum_a, sum_c, sum_vec = layer(
        n, lengths, tokens, cotangent, qkv_weight, out_weight, up_weight, down_weight, vec
    )
    down_sum = sum_a[:W]
    up_sum = sum_a[W : 2 * W].reshape(4, W // 4, W).transpose(1, 0, 2).reshape(W // 4, 4 * W)
    qkv_sum = sum_c[: 3 * W // 4].reshape(3, W // 4, W).transpose(1, 0, 2).reshape(W // 4, 3 * W)
    out_sum = sum_c[3 * W // 4 : W]
    vec_sum = lax.dynamic_slice(sum_vec.reshape(-1), (begin,), (share,))
    qkv_new = adamw(qkv_weight, qkv_first, qkv_second, qkv_sum, RATE_MATRIX)
    out_new = adamw(out_weight, out_first, out_second, out_sum, RATE_OUTPUT)
    up_new = adamw(up_weight, up_first, up_second, up_sum, RATE_MATRIX)
    down_new = adamw(down_weight, down_first, down_second, down_sum, RATE_MATRIX)
    vec_new = adamw(vectors, vectors_first, vectors_second, vec_sum, RATE_VECTOR)
    news = (qkv_new, out_new, up_new, down_new, vec_new)
    return (activations, input_grad) + tuple(new[i] for i in range(3) for new in news)


def solution(mesh):
    tokens = P(("dp", "zero"), None)
    params = (P("zero", None),) * 4 + (P("zero"),)
    return jax.shard_map(
        functools.partial(on_device, mesh.shape["dp"]),
        mesh=mesh,
        in_specs=(tokens,) * 3 + params * 3,
        out_specs=(tokens,) * 2 + params * 3,
        check_vma=False,
    )
```

```python
import functools
import math

import jax
import jax.numpy as jnp
from jax import lax
from jax.experimental import pallas as pl
from jax.experimental.pallas import tpu as pltpu
from jax.sharding import PartitionSpec as P

HEADS = 8
HEAD_DIM = 32
ROT = 8
STEP = 5


NORM_EPS = 1e-05
BETA_ONE = 0.9
BETA_TWO = 0.95
ADAM_EPS = 1e-08
DECAY = 0.01
RATE_MATRIX = 0.06
RATE_OUTPUT = 0.3
RATE_VECTOR = 0.5
NEGATIVE = -1e30
MESH = pl.DeviceIdType.MESH
F32 = jnp.float32
BF16 = jnp.bfloat16
VROWS = 32
W = 256


def adamw(master, first, second, grad, rate):
    momentum = BETA_ONE * first + (1.0 - BETA_ONE) * grad
    variance = BETA_TWO * second + (1.0 - BETA_TWO) * grad * grad
    direction = (
        momentum / (1.0 - BETA_ONE**STEP) / (jnp.sqrt(variance / (1.0 - BETA_TWO**STEP)) + ADAM_EPS)
    )
    return (master - rate * (direction + DECAY * master), momentum, variance)


def nn(a, b):
    return lax.dot_general(a, b, (((1,), (0,)), ((), ())), preferred_element_type=F32)


def nt(a, b):
    return lax.dot_general(a, b, (((1,), (1,)), ((), ())), preferred_element_type=F32)


def tn(a, b):
    return lax.dot_general(a, b, (((0,), (0,)), ((), ())), preferred_element_type=F32)


def remote(src, dst, send, recv, device):
    return pltpu.make_async_remote_copy(
        src_ref=src, dst_ref=dst, send_sem=send, recv_sem=recv, device_id=device, device_id_type=MESH
    )


class Reduction:
    def __init__(self, place, full, core_in, y_out, y_in, share, share_low, pieces, total, sems):
        self.place = place
        self.full, self.core_in, self.y_out, self.y_in = full, core_in, y_out, y_in
        self.share, self.share_low, self.pieces, self.total = share, share_low, pieces, total
        self.zs, self.zr, self.ds, self.dr, self.gs, self.gr = sems
        self.piece = pieces.shape[1]
        self.rows = full.shape[2]

    def core_copy(self, slot):
        p = self.place
        y = p.y if slot else 1 - p.y
        return remote(
            self.full.at[1 - p.c, y], self.core_in.at[y], self.zs.at[slot], self.zr.at[slot], {"zero": p.core}
        )

    def y_copy(self):
        return remote(self.y_out, self.y_in, self.zs.at[2], self.zr.at[2], {"zero": self.place.other})

    def rows_of(self, index):
        return pl.ds(pl.multiple_of(index * self.piece, self.piece), self.piece)

    def scatter_copy(self, k):
        p = self.place
        peer = lax.rem(p.dp + k, p.n)
        return remote(
            self.share_low.at[self.rows_of(peer)], self.pieces.at[k], self.ds.at[k], self.dr.at[k], {"dp": peer}
        )

    def gather_copy(self, k):
        p = self.place
        peer = lax.rem(p.dp + k, p.n)
        mine = self.total.at[self.rows_of(p.dp)]
        return remote(mine, mine, self.gs.at[k], self.gr.at[k], {"dp": peer})

    def gather_arrival(self, k):
        p = self.place
        peer = lax.rem(p.dp + p.n - k, p.n)
        theirs = self.total.at[self.rows_of(peer)]
        return remote(theirs, theirs, self.gs.at[k], self.gr.at[k], {"dp": peer})

    def loop(self, action):
        def body(k, carry):
            action(k)
            return carry

        lax.fori_loop(1, self.place.n, body, 0)

    def stage_core(self):
        self.core_copy(0).start()
        self.core_copy(1).start()

    def stage_y(self):
        p = self.place
        self.core_copy(0).wait_recv()
        self.y_out[...] = (self.full[p.c, 1 - p.y] + self.core_in[1 - p.y]).astype(BF16)
        self.y_copy().start()

    def stage_scatter(self):
        p = self.place
        self.core_copy(1).wait_recv()
        self.y_copy().wait_recv()
        summed = self.full[p.c, p.y] + self.core_in[p.y] + self.y_in[...].astype(F32)
        self.share[pl.ds(0, self.rows)] = summed
        self.share_low[pl.ds(0, self.rows)] = summed.astype(BF16)
        spare = self.share.shape[0] - self.rows
        if spare:
            self.share[pl.ds(self.rows, spare)] = jnp.zeros((spare, W), F32)
            self.share_low[pl.ds(self.rows, spare)] = jnp.zeros((spare, W), BF16)
        self.loop(lambda k: self.scatter_copy(k).start())

    def stage_gather(self):
        p = self.place
        self.loop(lambda k: self.scatter_copy(k).wait_recv())
        summed = self.share[self.rows_of(p.dp)]
        if p.n <= 16:
            for k in range(1, p.n):
                summed = summed + self.pieces[k].astype(F32)
        else:
            summed = lax.fori_loop(1, p.n, lambda k, s: s + self.pieces[k].astype(F32), summed)
        self.total[self.rows_of(p.dp)] = summed.astype(self.total.dtype)
        self.loop(lambda k: self.gather_copy(k).start())

    def stage_end(self):
        self.loop(lambda k: self.gather_arrival(k).wait_recv())

    def drain(self):
        self.core_copy(0).wait_send()
        self.core_copy(1).wait_send()
        self.y_copy().wait_send()
        self.loop(lambda k: self.scatter_copy(k).wait_send())
        self.loop(lambda k: self.gather_copy(k).wait_send())


class Place:
    def __init__(self, n):
        self.n = n
        self.dp = lax.axis_index("dp")
        self.z = lax.axis_index("zero")
        self.c = lax.rem(self.z, 2)
        self.y = self.z // 2
        self.core = 2 * self.y + 1 - self.c
        self.other = 2 * (1 - self.y) + self.c
        self.far = 2 * (1 - self.y) + 1 - self.c
        self.x = lax.rem(self.dp, 2)
        self.pair = self.dp + 1 - 2 * self.x


def layer_kernel(
    n,
    lengths, tokens, cotangent, qkv_s, out_s, up_s, down_s, vec_s,
    act_o, ig_o, gd_o, gu_o, gc_o, vec_o,
    qkv_w, out_w, up_w, down_w, vec_in, vec_g, vec_z, vec_t, vec_d,
    gat_s, gat_r, vs, vr, vds, vdr,
    bias_m, q_t, k_t, v_t, do_t, o_t, dlin_t, base, dh2_s,
    *groups,
):
    p = Place(n)
    count = tokens.shape[0]
    peers_zero = (p.core, p.other, p.far)
    group_d, group_u, group_c = (
        Reduction(p, *groups[14 * i : 14 * i + 8], groups[14 * i + 8 : 14 * i + 14]) for i in range(3)
    )
    d_full, u_full, c_full = group_d.full, group_u.full, group_c.full

    barrier = pltpu.get_barrier_semaphore()
    for peer in peers_zero:
        pl.semaphore_signal(barrier, inc=1, device_id={"zero": peer}, device_id_type=MESH)

    def greet(k, carry):
        peer = lax.rem(p.dp + k, n)
        pl.semaphore_signal(barrier, inc=1, device_id={"dp": peer}, device_id_type=MESH)
        return carry

    lax.fori_loop(1, n, greet, 0)

    first = lengths[0, 0]
    total = lengths[0, 0] + lengths[0, 1]
    index = lax.broadcasted_iota(jnp.int32, (1, count), 1)
    start = jnp.where(index >= total, total, jnp.where(index >= first, first, 0))
    live = jnp.where(index < total, 1.0, 0.0).astype(F32)
    key_index = lax.broadcasted_iota(jnp.int32, (count, count), 0)
    query_index = lax.broadcasted_iota(jnp.int32, (count, count), 1)
    bias_m[...] = jnp.where((key_index <= query_index) & (key_index >= start), 0.0, NEGATIVE).astype(F32)
    half = ROT // 2
    row = lax.broadcasted_iota(jnp.int32, (ROT, count), 0)
    turn = lax.rem(row, half)
    freq = jnp.where(turn == 0, 1.0, jnp.where(turn == 1, 0.1, jnp.where(turn == 2, 0.01, 0.001))).astype(F32)
    angle = (index - start).astype(F32) * freq
    cosine = jnp.cos(angle)
    sine = jnp.sin(angle) * jnp.where(row < half, -1.0, 1.0).astype(F32)

    def rotate(lines, signed):
        top = lines[:ROT]
        swapped = jnp.concatenate([top[half:], top[:half]], axis=0)
        return jnp.concatenate([top * cosine + swapped * signed, lines[ROT:]], axis=0)

    weights = (qkv_w, out_w, up_w, down_w)
    for buffer, shard in zip(weights, (qkv_s, out_s, up_s, down_s)):
        buffer[p.z] = shard[...].astype(BF16)
    pl.semaphore_wait(barrier, 3 + n - 1)

    def vec_copy(i, src, dst):
        return remote(src, dst.at[i], vs.at[i], vr.at[i], {"zero": peers_zero[i]})

    def shard_half(w, shard, half):
        rows = weights[w].shape[1] // 2
        return weights[w].at[shard, pl.ds(pl.multiple_of(half * rows, rows), rows)]

    def weight_moves(w, way, arrival):
        if way == 0:
            part = weights[w].at[p.core if arrival else p.z]
        elif way == 1:
            part = shard_half(w, p.other if arrival else p.z, p.x)
        elif way == 2:
            part = shard_half(w, p.other, 1 - p.x if arrival else p.x)
        else:
            part = shard_half(w, p.far if arrival else p.other, p.x if way == 3 else 1 - p.x)
        device = {1: {"zero": p.other}, 2: {"dp": p.pair}}.get(way, {"zero": p.core})
        return remote(part, part, gat_s.at[w, way], gat_r.at[w, way], device)

    def weight_copy(w, way):
        return weight_moves(w, way, False)

    def weight_arrival(w, way):
        return weight_moves(w, way, True)

    def relay_one(w):
        weight_arrival(w, 1).wait_recv()
        weight_copy(w, 2).start()
        weight_copy(w, 3).start()

    def relay_two(w):
        weight_arrival(w, 2).wait_recv()
        weight_copy(w, 4).start()

    def finish_weight(w):
        for way in (0, 3, 4):
            weight_arrival(w, way).wait_recv()

    for i in range(3):
        vec_copy(i, vec_s, vec_in).start()
    for w in (2, 3, 0, 1):
        weight_copy(w, 1).start()
        weight_copy(w, 0).start()

    x = tokens[...].astype(F32).T
    g = (cotangent[...].astype(F32).T * live).astype(BF16)
    centered = x - jnp.mean(x, axis=0, keepdims=True)
    rstd = lax.rsqrt(jnp.mean(centered * centered, axis=0, keepdims=True) + NORM_EPS)
    plain = centered * rstd

    for i in range(3):
        vec_copy(i, vec_s, vec_in).wait_recv()
    vec = (vec_s[...] + vec_in[0] + vec_in[1] + vec_in[2]).astype(BF16).astype(F32).T

    def column(begin, length):
        parts = [vec[:, i : i + 1] for i in range(begin // 128, (begin + length) // 128)]
        return jnp.concatenate(parts, axis=0)

    gain_one, bias_one, gain_two, bias_two = (column(W * i, W) for i in range(4))
    h1 = (plain * gain_one + bias_one).astype(BF16)
    h2 = (plain * gain_two + bias_two).astype(BF16)

    for w in (2, 3, 0, 1):
        relay_one(w)
    relay_two(2)
    relay_two(3)
    finish_weight(2)
    finish_weight(3)

    ones = jnp.ones((8, count), BF16)

    def put_sum(at, values):
        sums = nt(ones, values)
        for i in range(values.shape[0] // 128):
            vec_g[at // 128 + i : at // 128 + i + 1] = sums[0:1, 128 * i : 128 * i + 128]

    def put_sum_wide(at, values):
        high = values.astype(BF16)
        rest = (values - high.astype(F32)).astype(BF16)
        sums = nt(ones, high) + nt(ones, rest)
        for i in range(values.shape[0] // 128):
            vec_g[at // 128 + i : at // 128 + i + 1] = sums[0:1, 128 * i : 128 * i + 128]

    shard_rows = W // 4
    mlp = jnp.zeros((W, count), F32)
    dh2 = jnp.zeros((W, count), F32)
    for j in range(4):
        w_up = up_w[:, :, W * j : W * j + W].reshape(W, W)
        w_down = down_w[j]
        up = tn(w_up, h2) + column(8 * W + W * j, W)
        phi_sum = 0.5 + 0.5 * lax.erf(up * (0.5**0.5))
        z = (up * phi_sum).astype(BF16)
        bell = jnp.exp2(up * up * (-0.5 * math.log2(math.e))) * ((2.0 * math.pi) ** -0.5)
        du = (nn(w_down, g) * (phi_sum + up * bell)).astype(BF16)
        mlp = mlp + tn(w_down, z)
        dh2 = dh2 + nn(w_up, du)
        d_full[j % 2, j // 2] = nt(z, g)
        g_up = nt(h2, du)
        for s in range(4):
            u_full[s % 2, s // 2, pl.ds(shard_rows * j, shard_rows)] = g_up[shard_rows * s : shard_rows * (s + 1)]
        put_sum(8 * W + W * j, du)
        if j == 1:
            relay_two(0)
            relay_two(1)
    group_d.stage_core()
    group_u.stage_core()
    base[...] = x + mlp + column(12 * W, W)
    dh2_s[...] = dh2

    scale = HEAD_DIM**-0.5
    finish_weight(0)
    for part, target in enumerate((q_t, k_t, v_t)):
        block = qkv_w[:, :, W * part : W * part + W].reshape(W, W)
        lines = tn(block, h1) + column(4 * W + W * part, W)
        for h in range(HEADS):
            piece = lines[HEAD_DIM * h : HEAD_DIM * h + HEAD_DIM]
            if part < 2:
                piece = rotate(piece, sine)
            target[HEAD_DIM * h : HEAD_DIM * h + HEAD_DIM] = piece.astype(BF16)
    finish_weight(1)
    do_t[...] = nn(out_w[...].reshape(W, W), g).astype(BF16)

    group_d.stage_y()
    group_u.stage_y()

    fold = scale * math.log2(math.e)
    block = count // 2

    def head(h, carry):
        at = pl.ds(pl.multiple_of(h * HEAD_DIM, HEAD_DIM), HEAD_DIM)
        q, k, v, do = q_t[at], k_t[at], v_t[at], do_t[at]
        outs, dqs, dks, dvs = [], [], [], []
        for j in range(2):
            keys = block * (j + 1)
            cut = slice(block * j, block * (j + 1))
            kk, vv, qj, dj = k[:, :keys], v[:, :keys], q[:, cut], do[:, cut]
            scores = tn(kk, qj) * fold + bias_m[:keys, cut]
            raised = jnp.exp2(scores - jnp.max(scores, axis=0, keepdims=True))
            chances = raised * (1.0 / jnp.sum(raised, axis=0, keepdims=True))
            low = chances.astype(BF16)
            outs.append(nn(vv, low))
            inner = tn(vv, dj)
            slope = (chances * (inner - jnp.sum(inner * chances, axis=0, keepdims=True))).astype(BF16)
            dqs.append(nn(kk, slope))
            dks.append(nt(qj, slope))
            dvs.append(nt(dj, low))
        o_t[at] = jnp.concatenate(outs, axis=1).astype(BF16)
        dq = jnp.concatenate(dqs, axis=1) * scale
        dk = jnp.concatenate([dks[0] + dks[1][:, :block], dks[1][:, block:]], axis=1) * scale
        dv = jnp.concatenate([dvs[0] + dvs[1][:, :block], dvs[1][:, block:]], axis=1)
        dlin_t[0, at] = rotate(dq, -sine).astype(BF16)
        dlin_t[1, at] = rotate(dk, -sine).astype(BF16)
        dlin_t[2, at] = dv.astype(BF16)
        return carry

    lax.fori_loop(0, 2, head, 0)
    group_d.stage_scatter()
    lax.fori_loop(2, 4, head, 0)
    group_u.stage_scatter()
    group_d.stage_gather()
    lax.fori_loop(4, 6, head, 0)
    group_u.stage_gather()
    lax.fori_loop(6, 8, head, 0)

    for j in range(3):
        dlin = dlin_t[j]
        g_qkv = nt(h1, dlin)
        for s in range(4):
            c_full[s % 2, s // 2, pl.ds(shard_rows * j, shard_rows)] = g_qkv[shard_rows * s : shard_rows * (s + 1)]
        put_sum(4 * W + W * j, dlin)
    g_out = nt(o_t[...], g)
    for s in range(4):
        c_full[s % 2, s // 2, pl.ds(3 * shard_rows, shard_rows)] = g_out[shard_rows * s : shard_rows * (s + 1)]
    group_c.stage_core()

    dh1 = jnp.zeros((W, count), F32)
    for j in range(3):
        dh1 = dh1 + nn(qkv_w[:, :, W * j : W * j + W].reshape(W, W), dlin_t[j])
    group_c.stage_y()
    dh2 = dh2_s[...]
    put_sum_wide(0, dh1 * plain)
    put_sum_wide(W, dh1)
    put_sum_wide(2 * W, dh2 * plain)
    put_sum_wide(3 * W, dh2)
    put_sum(7 * W, g)
    put_sum(12 * W, g)
    vec_g[13 * W // 128 : VROWS] = jnp.zeros((VROWS - 13 * W // 128, 128), F32)

    def vec_zero(i):
        return remote(vec_g, vec_z.at[i], vs.at[3 + i], vr.at[3 + i], {"zero": peers_zero[i]})

    for i in range(3):
        vec_zero(i).start()
    group_c.stage_scatter()
    dn = dh1 * gain_one + dh2 * gain_two
    term = (
        dn - jnp.mean(dn, axis=0, keepdims=True) - plain * jnp.mean(dn * plain, axis=0, keepdims=True)
    ) * rstd
    for i in range(3):
        vec_zero(i).wait_recv()
    vec_t[...] = vec_g[...] + vec_z[0] + vec_z[1] + vec_z[2]

    def vec_dp(k):
        peer = lax.rem(p.dp + k, n)
        return remote(vec_t, vec_d.at[k], vds.at[k], vdr.at[k], {"dp": peer})

    group_c.loop(lambda k: vec_dp(k).start())
    ig_o[...] = (g.astype(F32) + term).T.astype(BF16)
    attn = tn(out_w[...].reshape(W, W), o_t[...]) + column(7 * W, W)
    act_o[...] = ((base[...] + attn) * live).T.astype(BF16)

    group_c.stage_gather()
    group_d.stage_end()
    gd_o[...] = group_d.total[...]
    group_u.stage_end()
    gu_o[...] = group_u.total[...]
    group_c.loop(lambda k: vec_dp(k).wait_recv())
    vec_o[...] = lax.fori_loop(1, n, lambda k, s: s + vec_d[k], vec_t[...])
    for w in range(4):
        for way in range(5):
            weight_copy(w, way).wait_send()
    for i in range(3):
        vec_copy(i, vec_s, vec_in).wait_send()
        vec_zero(i).wait_send()
    group_c.loop(lambda k: vec_dp(k).wait_send())
    group_d.drain()
    group_u.drain()
    group_c.stage_end()
    gc_o[...] = group_c.total[...]
    group_c.drain()


def piece_rows(rows, n):
    return -(-rows // (16 * n)) * 16


def reduction_scratch(rows, n, kind):
    piece = piece_rows(rows, n)
    dma = pltpu.SemaphoreType.DMA
    return [
        pltpu.VMEM((2, 2, rows, W), F32),
        pltpu.VMEM((2, rows, W), F32),
        pltpu.VMEM((rows, W), BF16),
        pltpu.VMEM((rows, W), BF16),
        pltpu.VMEM((n * piece, W), F32),
        pltpu.VMEM((n * piece, W), BF16),
        pltpu.VMEM((n, piece, W), BF16),
        pltpu.VMEM((n * piece, W), kind),
        dma((3,)), dma((3,)), dma((n,)), dma((n,)), dma((n,)), dma((n,)),
    ]


def layer(n, lengths, tokens, cotangent, qkv, out, up, down, vec):
    count = tokens.shape[0]
    dma = pltpu.SemaphoreType.DMA
    rows = n * piece_rows(256, n)
    vmem = pl.BlockSpec(memory_space=pltpu.VMEM)
    return pl.pallas_call(
        functools.partial(layer_kernel, n),
        out_shape=(
            jax.ShapeDtypeStruct(tokens.shape, BF16),
            jax.ShapeDtypeStruct(tokens.shape, BF16),
            jax.ShapeDtypeStruct((rows, W), BF16),
            jax.ShapeDtypeStruct((rows, W), BF16),
            jax.ShapeDtypeStruct((rows, W), BF16),
            jax.ShapeDtypeStruct((VROWS, 128), F32),
        ),
        in_specs=[pl.BlockSpec(memory_space=pltpu.SMEM)] + [vmem] * 7,
        out_specs=[vmem] * 6,
        scratch_shapes=[
            pltpu.VMEM((4, 64, 3 * W), BF16),
            pltpu.VMEM((4, 64, W), BF16),
            pltpu.VMEM((4, 64, 4 * W), BF16),
            pltpu.VMEM((4, W, W), BF16),
            pltpu.VMEM((3, VROWS, 128), F32),
            pltpu.VMEM((VROWS, 128), F32),
            pltpu.VMEM((3, VROWS, 128), F32),
            pltpu.VMEM((VROWS, 128), F32),
            pltpu.VMEM((n, VROWS, 128), F32),
            dma((4, 5)), dma((4, 5)), dma((6,)), dma((6,)), dma((n,)), dma((n,)),
            pltpu.VMEM((count, count), F32),
            pltpu.VMEM((W, count), BF16),
            pltpu.VMEM((W, count), BF16),
            pltpu.VMEM((W, count), BF16),
            pltpu.VMEM((W, count), BF16),
            pltpu.VMEM((W, count), BF16),
            pltpu.VMEM((3, W, count), BF16),
            pltpu.VMEM((W, count), F32),
            pltpu.VMEM((W, count), F32),
        ]
        + reduction_scratch(W, n, BF16) * 3,
        compiler_params=pltpu.CompilerParams(
            collective_id=0, has_side_effects=True, vmem_limit_bytes=56 * 1024 * 1024
        ),
        name="layer",
    )(lengths, tokens, cotangent, qkv, out, up, down, vec)


RATES = (RATE_MATRIX, RATE_OUTPUT, RATE_MATRIX, RATE_MATRIX)


def update_kernel(*refs):
    passed, sums, states = refs[0:2], refs[2:5], refs[5:17]
    passed_o, states_o = refs[17:19], refs[19:31]
    sums_v, ins, outs = refs[31:34], refs[34:46], refs[46:58]
    held = refs[58:60]
    pass_sem, sum_sem, in_sem, out_sem = refs[60:64]
    order = (3, 2, 0, 1)
    through_in = [pltpu.make_async_copy(passed[i], held[i], pass_sem.at[i]) for i in range(2)]
    through = [pltpu.make_async_copy(held[i], passed_o[i], pass_sem.at[2 + i]) for i in range(2)]
    sum_in = [pltpu.make_async_copy(sums[i], sums_v[i], sum_sem.at[i]) for i in range(3)]
    copy_in = [pltpu.make_async_copy(states[i], ins[i], in_sem.at[i]) for i in range(12)]
    copy_out = [pltpu.make_async_copy(outs[i], states_o[i], out_sem.at[i]) for i in range(12)]
    for copy in sum_in:
        copy.start()
    for w in order:
        for kind in range(3):
            copy_in[4 * kind + w].start()
    for copy in through_in:
        copy.start()
    for copy in sum_in:
        copy.wait()
    quarter = W // 4
    for w in order:
        if w == 2:
            for i in range(2):
                through_in[i].wait()
                through[i].start()
        for kind in range(3):
            copy_in[4 * kind + w].wait()
        rows, columns = ins[w].shape
        begin = (0, 3 * quarter, 0, 0)[w]
        group = sums_v[(2, 2, 1, 0)[w]]
        for j in range(columns // W):
            cut = slice(W * j, W * j + W)
            grad = group[begin + rows * j : begin + rows * j + rows].astype(F32)
            new = adamw(ins[w][:, cut], ins[4 + w][:, cut], ins[8 + w][:, cut], grad, RATES[w])
            for kind in range(3):
                outs[4 * kind + w][:, cut] = new[kind]
        for kind in range(3):
            copy_out[4 * kind + w].start()
    for copy in copy_out + through:
        copy.wait()


def update(activations, input_grad, sums, states):
    hbm = pl.BlockSpec(memory_space=pl.ANY)
    shapes = [jax.ShapeDtypeStruct(a.shape, a.dtype) for a in (activations, input_grad) + states]
    dma = pltpu.SemaphoreType.DMA
    return pl.pallas_call(
        update_kernel,
        out_shape=shapes,
        in_specs=[hbm] * 17,
        out_specs=[hbm] * 14,
        scratch_shapes=[pltpu.VMEM(a.shape, a.dtype) for a in sums + states + states + (activations, input_grad)]
        + [dma((4,)), dma((3,)), dma((12,)), dma((12,))],
        compiler_params=pltpu.CompilerParams(vmem_limit_bytes=56 * 1024 * 1024),
        name="update",
    )(activations, input_grad, *sums, *states)


def on_device(
    n,
    tokens,
    cotangent,
    lengths,
    qkv_weight,
    out_weight,
    up_weight,
    down_weight,
    vectors,
    qkv_first,
    out_first,
    up_first,
    down_first,
    vectors_first,
    qkv_second,
    out_second,
    up_second,
    down_second,
    vectors_second,
):
    share = vectors.shape[0]
    begin = lax.axis_index("zero") * share
    vec = lax.dynamic_update_slice(jnp.zeros((VROWS * 128,), F32), vectors, (begin,)).reshape(VROWS, 128)
    activations, input_grad, *sums, sum_vec = layer(
        n, lengths, tokens, cotangent, qkv_weight, out_weight, up_weight, down_weight, vec
    )
    vec_sum = lax.dynamic_slice(sum_vec.reshape(-1), (begin,), (share,))
    vec_new = adamw(vectors, vectors_first, vectors_second, vec_sum, RATE_VECTOR)
    states = (
        qkv_weight, out_weight, up_weight, down_weight,
        qkv_first, out_first, up_first, down_first,
        qkv_second, out_second, up_second, down_second,
    )
    news = update(activations, input_grad, tuple(sums), states)
    return (
        *news[0:6], vec_new[0], *news[6:10], vec_new[1], *news[10:14], vec_new[2],
    )


def solution(mesh):
    tokens = P(("dp", "zero"), None)
    params = (P("zero", None),) * 4 + (P("zero"),)
    return jax.shard_map(
        functools.partial(on_device, mesh.shape["dp"]),
        mesh=mesh,
        in_specs=(tokens,) * 3 + params * 3,
        out_specs=(tokens,) * 2 + params * 3,
        check_vma=False,
    )
```

```python
import functools
import math

import jax
import jax.numpy as jnp
from jax import lax
from jax.experimental import pallas as pl
from jax.experimental.pallas import tpu as pltpu
from jax.sharding import PartitionSpec as P

HEADS = 8
HEAD_DIM = 32
ROT = 8
STEP = 5


NORM_EPS = 1e-05
BETA_ONE = 0.9
BETA_TWO = 0.95
ADAM_EPS = 1e-08
DECAY = 0.01
RATE_MATRIX = 0.06
RATE_OUTPUT = 0.3
RATE_VECTOR = 0.5
NEGATIVE = -1e30
MESH = pl.DeviceIdType.MESH
F32 = jnp.float32
BF16 = jnp.bfloat16
VROWS = 32
W = 256


def adamw(master, first, second, grad, rate):
    momentum = BETA_ONE * first + (1.0 - BETA_ONE) * grad
    variance = BETA_TWO * second + (1.0 - BETA_TWO) * grad * grad
    direction = (
        momentum / (1.0 - BETA_ONE**STEP) / (jnp.sqrt(variance / (1.0 - BETA_TWO**STEP)) + ADAM_EPS)
    )
    return (master - rate * (direction + DECAY * master), momentum, variance)


def nn(a, b):
    return lax.dot_general(a, b, (((1,), (0,)), ((), ())), preferred_element_type=F32)


def nt(a, b):
    return lax.dot_general(a, b, (((1,), (1,)), ((), ())), preferred_element_type=F32)


def tn(a, b):
    return lax.dot_general(a, b, (((0,), (0,)), ((), ())), preferred_element_type=F32)


def remote(src, dst, send, recv, device):
    return pltpu.make_async_remote_copy(
        src_ref=src, dst_ref=dst, send_sem=send, recv_sem=recv, device_id=device, device_id_type=MESH
    )


class Reduction:
    def __init__(self, place, full, core_in, y_out, y_in, share, share_low, pieces, total, sems):
        self.place = place
        self.full, self.core_in, self.y_out, self.y_in = full, core_in, y_out, y_in
        self.share, self.share_low, self.pieces, self.total = share, share_low, pieces, total
        self.zs, self.zr, self.ds, self.dr, self.gs, self.gr = sems
        self.piece = pieces.shape[1]
        self.rows = full.shape[2]

    def core_copy(self, slot):
        p = self.place
        y = p.y if slot else 1 - p.y
        return remote(
            self.full.at[1 - p.c, y], self.core_in.at[y], self.zs.at[slot], self.zr.at[slot], {"zero": p.core}
        )

    def y_copy(self):
        return remote(self.y_out, self.y_in, self.zs.at[2], self.zr.at[2], {"zero": self.place.other})

    def rows_of(self, index):
        return pl.ds(pl.multiple_of(index * self.piece, self.piece), self.piece)

    def scatter_copy(self, k):
        p = self.place
        peer = lax.rem(p.dp + k, p.n)
        return remote(
            self.share_low.at[self.rows_of(peer)], self.pieces.at[k], self.ds.at[k], self.dr.at[k], {"dp": peer}
        )

    def gather_copy(self, k):
        p = self.place
        peer = lax.rem(p.dp + k, p.n)
        mine = self.total.at[self.rows_of(p.dp)]
        return remote(mine, mine, self.gs.at[k], self.gr.at[k], {"dp": peer})

    def gather_arrival(self, k):
        p = self.place
        peer = lax.rem(p.dp + p.n - k, p.n)
        theirs = self.total.at[self.rows_of(peer)]
        return remote(theirs, theirs, self.gs.at[k], self.gr.at[k], {"dp": peer})

    def loop(self, action):
        def body(k, carry):
            action(k)
            return carry

        lax.fori_loop(1, self.place.n, body, 0)

    def stage_core(self):
        self.core_copy(0).start()
        self.core_copy(1).start()

    def stage_y(self):
        p = self.place
        self.core_copy(0).wait_recv()
        self.y_out[...] = (self.full[p.c, 1 - p.y] + self.core_in[1 - p.y]).astype(BF16)
        self.y_copy().start()

    def stage_scatter(self):
        p = self.place
        self.core_copy(1).wait_recv()
        self.y_copy().wait_recv()
        summed = self.full[p.c, p.y] + self.core_in[p.y] + self.y_in[...].astype(F32)
        self.share[pl.ds(0, self.rows)] = summed
        self.share_low[pl.ds(0, self.rows)] = summed.astype(BF16)
        spare = self.share.shape[0] - self.rows
        if spare:
            self.share[pl.ds(self.rows, spare)] = jnp.zeros((spare, W), F32)
            self.share_low[pl.ds(self.rows, spare)] = jnp.zeros((spare, W), BF16)
        self.loop(lambda k: self.scatter_copy(k).start())

    def stage_gather(self):
        p = self.place
        self.loop(lambda k: self.scatter_copy(k).wait_recv())
        summed = self.share[self.rows_of(p.dp)]
        if p.n <= 16:
            for k in range(1, p.n):
                summed = summed + self.pieces[k].astype(F32)
        else:
            summed = lax.fori_loop(1, p.n, lambda k, s: s + self.pieces[k].astype(F32), summed)
        self.total[self.rows_of(p.dp)] = summed.astype(self.total.dtype)
        self.loop(lambda k: self.gather_copy(k).start())

    def stage_end(self):
        self.loop(lambda k: self.gather_arrival(k).wait_recv())

    def drain(self):
        self.core_copy(0).wait_send()
        self.core_copy(1).wait_send()
        self.y_copy().wait_send()
        self.loop(lambda k: self.scatter_copy(k).wait_send())
        self.loop(lambda k: self.gather_copy(k).wait_send())


class Place:
    def __init__(self, n):
        self.n = n
        self.dp = lax.axis_index("dp")
        self.z = lax.axis_index("zero")
        self.c = lax.rem(self.z, 2)
        self.y = self.z // 2
        self.core = 2 * self.y + 1 - self.c
        self.other = 2 * (1 - self.y) + self.c
        self.far = 2 * (1 - self.y) + 1 - self.c
        self.x = lax.rem(self.dp, 2)
        self.pair = self.dp + 1 - 2 * self.x


def layer_kernel(
    n,
    lengths, tokens, cotangent, qkv_s, out_s, up_s, down_s, vec_s,
    act_o, ig_o, gd_o, gu_o, gc_o, vec_o,
    qkv_w, out_w, up_w, down_w, vec_in, vec_g, vec_z, vec_t, vec_d,
    gat_s, gat_r, vs, vr, vds, vdr,
    bias_m, q_t, k_t, v_t, do_t, o_t, dlin_t, base, dh2_s,
    *groups,
):
    p = Place(n)
    count = tokens.shape[0]
    peers_zero = (p.core, p.other, p.far)
    group_d, group_u, group_c = (
        Reduction(p, *groups[14 * i : 14 * i + 8], groups[14 * i + 8 : 14 * i + 14]) for i in range(3)
    )
    d_full, u_full, c_full = group_d.full, group_u.full, group_c.full

    barrier = pltpu.get_barrier_semaphore()
    for peer in peers_zero:
        pl.semaphore_signal(barrier, inc=1, device_id={"zero": peer}, device_id_type=MESH)

    def greet(k, carry):
        peer = lax.rem(p.dp + k, n)
        pl.semaphore_signal(barrier, inc=1, device_id={"dp": peer}, device_id_type=MESH)
        return carry

    lax.fori_loop(1, n, greet, 0)

    first = lengths[0, 0]
    total = lengths[0, 0] + lengths[0, 1]
    index = lax.broadcasted_iota(jnp.int32, (1, count), 1)
    start = jnp.where(index >= total, total, jnp.where(index >= first, first, 0))
    live = jnp.where(index < total, 1.0, 0.0).astype(F32)
    key_index = lax.broadcasted_iota(jnp.int32, (count, count), 0)
    query_index = lax.broadcasted_iota(jnp.int32, (count, count), 1)
    bias_m[...] = jnp.where((key_index <= query_index) & (key_index >= start), 0.0, NEGATIVE).astype(F32)
    half = ROT // 2
    row = lax.broadcasted_iota(jnp.int32, (ROT, count), 0)
    turn = lax.rem(row, half)
    freq = jnp.where(turn == 0, 1.0, jnp.where(turn == 1, 0.1, jnp.where(turn == 2, 0.01, 0.001))).astype(F32)
    angle = (index - start).astype(F32) * freq
    cosine = jnp.cos(angle)
    sine = jnp.sin(angle) * jnp.where(row < half, -1.0, 1.0).astype(F32)

    def rotate(lines, signed):
        top = lines[:ROT]
        swapped = jnp.concatenate([top[half:], top[:half]], axis=0)
        return jnp.concatenate([top * cosine + swapped * signed, lines[ROT:]], axis=0)

    weights = (qkv_w, out_w, up_w, down_w)
    for buffer, shard in zip(weights, (qkv_s, out_s, up_s, down_s)):
        buffer[p.z] = shard[...].astype(BF16)
    pl.semaphore_wait(barrier, 3 + n - 1)

    def vec_copy(i, src, dst):
        return remote(src, dst.at[i], vs.at[i], vr.at[i], {"zero": peers_zero[i]})

    ways = ((0, 1, 3), (0, 1, 3), (0, 1, 2, 3, 4), (0, 1, 2, 3, 4))

    def shard_half(w, shard, half):
        if w < 2:
            return weights[w].at[shard]
        rows = weights[w].shape[1] // 2
        return weights[w].at[shard, pl.ds(pl.multiple_of(half * rows, rows), rows)]

    def weight_moves(w, way, arrival):
        if way == 0:
            part = weights[w].at[p.core if arrival else p.z]
        elif way == 1:
            part = shard_half(w, p.other if arrival else p.z, p.x)
        elif way == 2:
            part = shard_half(w, p.other, 1 - p.x if arrival else p.x)
        else:
            part = shard_half(w, p.far if arrival else p.other, p.x if way == 3 else 1 - p.x)
        device = {1: {"zero": p.other}, 2: {"dp": p.pair}}.get(way, {"zero": p.core})
        return remote(part, part, gat_s.at[w, way], gat_r.at[w, way], device)

    def weight_copy(w, way):
        return weight_moves(w, way, False)

    def weight_arrival(w, way):
        return weight_moves(w, way, True)

    def relay_one(w):
        weight_arrival(w, 1).wait_recv()
        if w >= 2:
            weight_copy(w, 2).start()
        weight_copy(w, 3).start()

    def relay_two(w):
        weight_arrival(w, 2).wait_recv()
        weight_copy(w, 4).start()

    def finish_weight(w):
        for way in ways[w]:
            if way in (0, 3, 4):
                weight_arrival(w, way).wait_recv()

    for i in range(3):
        vec_copy(i, vec_s, vec_in).start()
    for w in range(2):
        weight_copy(w, 1).start()
        weight_copy(w, 0).start()

    x = tokens[...].astype(F32).T
    g = (cotangent[...].astype(F32).T * live).astype(BF16)
    centered = x - jnp.mean(x, axis=0, keepdims=True)
    rstd = lax.rsqrt(jnp.mean(centered * centered, axis=0, keepdims=True) + NORM_EPS)
    plain = centered * rstd

    for i in range(3):
        vec_copy(i, vec_s, vec_in).wait_recv()
    vec = (vec_s[...] + vec_in[0] + vec_in[1] + vec_in[2]).astype(BF16).astype(F32).T

    def column(begin, length):
        parts = [vec[:, i : i + 1] for i in range(begin // 128, (begin + length) // 128)]
        return jnp.concatenate(parts, axis=0)

    gain_one, bias_one, gain_two, bias_two = (column(W * i, W) for i in range(4))
    h1 = (plain * gain_one + bias_one).astype(BF16)
    h2 = (plain * gain_two + bias_two).astype(BF16)

    relay_one(0)
    relay_one(1)
    for w in (2, 3):
        weight_copy(w, 1).start()
        weight_copy(w, 0).start()

    scale = HEAD_DIM**-0.5
    finish_weight(0)
    for part, target in enumerate((q_t, k_t, v_t)):
        block = qkv_w[:, :, W * part : W * part + W].reshape(W, W)
        lines = tn(block, h1) + column(4 * W + W * part, W)
        for h in range(HEADS):
            piece = lines[HEAD_DIM * h : HEAD_DIM * h + HEAD_DIM]
            if part < 2:
                piece = rotate(piece, sine)
            target[HEAD_DIM * h : HEAD_DIM * h + HEAD_DIM] = piece.astype(BF16)
    finish_weight(1)
    do_t[...] = nn(out_w[...].reshape(W, W), g).astype(BF16)

    fold = scale * math.log2(math.e)
    block = count // 2

    def head(h, carry):
        at = pl.ds(pl.multiple_of(h * HEAD_DIM, HEAD_DIM), HEAD_DIM)
        q, k, v, do = q_t[at], k_t[at], v_t[at], do_t[at]
        outs, dqs, dks, dvs = [], [], [], []
        for j in range(2):
            keys = block * (j + 1)
            cut = slice(block * j, block * (j + 1))
            kk, vv, qj, dj = k[:, :keys], v[:, :keys], q[:, cut], do[:, cut]
            scores = tn(kk, qj) * fold + bias_m[:keys, cut]
            raised = jnp.exp2(scores - jnp.max(scores, axis=0, keepdims=True))
            chances = raised * (1.0 / jnp.sum(raised, axis=0, keepdims=True))
            low = chances.astype(BF16)
            outs.append(nn(vv, low))
            inner = tn(vv, dj)
            slope = (chances * (inner - jnp.sum(inner * chances, axis=0, keepdims=True))).astype(BF16)
            dqs.append(nn(kk, slope))
            dks.append(nt(qj, slope))
            dvs.append(nt(dj, low))
        o_t[at] = jnp.concatenate(outs, axis=1).astype(BF16)
        dq = jnp.concatenate(dqs, axis=1) * scale
        dk = jnp.concatenate([dks[0] + dks[1][:, :block], dks[1][:, block:]], axis=1) * scale
        dv = jnp.concatenate([dvs[0] + dvs[1][:, :block], dvs[1][:, block:]], axis=1)
        dlin_t[0, at] = rotate(dq, -sine).astype(BF16)
        dlin_t[1, at] = rotate(dk, -sine).astype(BF16)
        dlin_t[2, at] = dv.astype(BF16)
        return carry

    relay_one(2)
    relay_one(3)
    lax.fori_loop(0, 2, head, 0, unroll=True)
    relay_two(2)
    relay_two(3)
    lax.fori_loop(2, 4, head, 0, unroll=True)
    finish_weight(2)
    finish_weight(3)

    ones = jnp.ones((8, count), BF16)

    def put_sum(at, values):
        sums = nt(ones, values)
        for i in range(values.shape[0] // 128):
            vec_g[at // 128 + i : at // 128 + i + 1] = sums[0:1, 128 * i : 128 * i + 128]

    def put_sum_wide(at, values):
        high = values.astype(BF16)
        rest = (values - high.astype(F32)).astype(BF16)
        sums = nt(ones, high) + nt(ones, rest)
        for i in range(values.shape[0] // 128):
            vec_g[at // 128 + i : at // 128 + i + 1] = sums[0:1, 128 * i : 128 * i + 128]

    shard_rows = W // 4
    mlp = jnp.zeros((W, count), F32)
    dh2 = jnp.zeros((W, count), F32)
    for j in range(4):
        w_up = up_w[:, :, W * j : W * j + W].reshape(W, W)
        w_down = down_w[j]
        up = tn(w_up, h2) + column(8 * W + W * j, W)
        phi_sum = 0.5 + 0.5 * lax.erf(up * (0.5**0.5))
        z = (up * phi_sum).astype(BF16)
        bell = jnp.exp2(up * up * (-0.5 * math.log2(math.e))) * ((2.0 * math.pi) ** -0.5)
        du = (nn(w_down, g) * (phi_sum + up * bell)).astype(BF16)
        mlp = mlp + tn(w_down, z)
        dh2 = dh2 + nn(w_up, du)
        d_full[j % 2, j // 2] = nt(z, g)
        g_up = nt(h2, du)
        for s in range(4):
            u_full[s % 2, s // 2, pl.ds(shard_rows * j, shard_rows)] = g_up[shard_rows * s : shard_rows * (s + 1)]
        put_sum(8 * W + W * j, du)
    group_d.stage_core()
    group_u.stage_core()
    base[...] = x + mlp + column(12 * W, W)
    dh2_s[...] = dh2
    group_d.stage_y()
    group_u.stage_y()

    lax.fori_loop(4, 6, head, 0, unroll=True)
    group_d.stage_scatter()
    group_u.stage_scatter()
    lax.fori_loop(6, 8, head, 0, unroll=True)
    group_d.stage_gather()

    for j in range(3):
        dlin = dlin_t[j]
        g_qkv = nt(h1, dlin)
        for s in range(4):
            c_full[s % 2, s // 2, pl.ds(shard_rows * j, shard_rows)] = g_qkv[shard_rows * s : shard_rows * (s + 1)]
        put_sum(4 * W + W * j, dlin)
    g_out = nt(o_t[...], g)
    for s in range(4):
        c_full[s % 2, s // 2, pl.ds(3 * shard_rows, shard_rows)] = g_out[shard_rows * s : shard_rows * (s + 1)]
    group_c.stage_core()
    group_u.stage_gather()

    dh1 = jnp.zeros((W, count), F32)
    for j in range(3):
        dh1 = dh1 + nn(qkv_w[:, :, W * j : W * j + W].reshape(W, W), dlin_t[j])
    group_c.stage_y()
    dh2 = dh2_s[...]
    put_sum_wide(0, dh1 * plain)
    put_sum_wide(W, dh1)
    put_sum_wide(2 * W, dh2 * plain)
    put_sum_wide(3 * W, dh2)
    put_sum(7 * W, g)
    put_sum(12 * W, g)
    vec_g[13 * W // 128 : VROWS] = jnp.zeros((VROWS - 13 * W // 128, 128), F32)

    def vec_zero(i):
        return remote(vec_g, vec_z.at[i], vs.at[3 + i], vr.at[3 + i], {"zero": peers_zero[i]})

    for i in range(3):
        vec_zero(i).start()
    group_c.stage_scatter()
    dn = dh1 * gain_one + dh2 * gain_two
    term = (
        dn - jnp.mean(dn, axis=0, keepdims=True) - plain * jnp.mean(dn * plain, axis=0, keepdims=True)
    ) * rstd
    for i in range(3):
        vec_zero(i).wait_recv()
    vec_t[...] = vec_g[...] + vec_z[0] + vec_z[1] + vec_z[2]

    def vec_dp(k):
        peer = lax.rem(p.dp + k, n)
        return remote(vec_t, vec_d.at[k], vds.at[k], vdr.at[k], {"dp": peer})

    group_c.loop(lambda k: vec_dp(k).start())
    ig_o[...] = (g.astype(F32) + term).T.astype(BF16)
    attn = tn(out_w[...].reshape(W, W), o_t[...]) + column(7 * W, W)
    act_o[...] = ((base[...] + attn) * live).T.astype(BF16)

    group_c.stage_gather()
    group_d.stage_end()
    gd_o[...] = group_d.total[...]
    group_u.stage_end()
    gu_o[...] = group_u.total[...]
    group_c.loop(lambda k: vec_dp(k).wait_recv())
    vec_o[...] = lax.fori_loop(1, n, lambda k, s: s + vec_d[k], vec_t[...])
    for w in range(4):
        for way in ways[w]:
            weight_copy(w, way).wait_send()
    for i in range(3):
        vec_copy(i, vec_s, vec_in).wait_send()
        vec_zero(i).wait_send()
    group_c.loop(lambda k: vec_dp(k).wait_send())
    group_d.drain()
    group_u.drain()
    group_c.stage_end()
    gc_o[...] = group_c.total[...]
    group_c.drain()


def piece_rows(rows, n):
    return -(-rows // (16 * n)) * 16


def reduction_scratch(rows, n, kind):
    piece = piece_rows(rows, n)
    dma = pltpu.SemaphoreType.DMA
    return [
        pltpu.VMEM((2, 2, rows, W), F32),
        pltpu.VMEM((2, rows, W), F32),
        pltpu.VMEM((rows, W), BF16),
        pltpu.VMEM((rows, W), BF16),
        pltpu.VMEM((n * piece, W), F32),
        pltpu.VMEM((n * piece, W), BF16),
        pltpu.VMEM((n, piece, W), BF16),
        pltpu.VMEM((n * piece, W), kind),
        dma((3,)), dma((3,)), dma((n,)), dma((n,)), dma((n,)), dma((n,)),
    ]


def layer(n, lengths, tokens, cotangent, qkv, out, up, down, vec):
    count = tokens.shape[0]
    dma = pltpu.SemaphoreType.DMA
    rows = n * piece_rows(256, n)
    vmem = pl.BlockSpec(memory_space=pltpu.VMEM)
    return pl.pallas_call(
        functools.partial(layer_kernel, n),
        out_shape=(
            jax.ShapeDtypeStruct(tokens.shape, BF16),
            jax.ShapeDtypeStruct(tokens.shape, BF16),
            jax.ShapeDtypeStruct((rows, W), BF16),
            jax.ShapeDtypeStruct((rows, W), BF16),
            jax.ShapeDtypeStruct((rows, W), BF16),
            jax.ShapeDtypeStruct((VROWS, 128), F32),
        ),
        in_specs=[pl.BlockSpec(memory_space=pltpu.SMEM)] + [vmem] * 7,
        out_specs=[vmem] * 6,
        scratch_shapes=[
            pltpu.VMEM((4, 64, 3 * W), BF16),
            pltpu.VMEM((4, 64, W), BF16),
            pltpu.VMEM((4, 64, 4 * W), BF16),
            pltpu.VMEM((4, W, W), BF16),
            pltpu.VMEM((3, VROWS, 128), F32),
            pltpu.VMEM((VROWS, 128), F32),
            pltpu.VMEM((3, VROWS, 128), F32),
            pltpu.VMEM((VROWS, 128), F32),
            pltpu.VMEM((n, VROWS, 128), F32),
            dma((4, 5)), dma((4, 5)), dma((6,)), dma((6,)), dma((n,)), dma((n,)),
            pltpu.VMEM((count, count), F32),
            pltpu.VMEM((W, count), BF16),
            pltpu.VMEM((W, count), BF16),
            pltpu.VMEM((W, count), BF16),
            pltpu.VMEM((W, count), BF16),
            pltpu.VMEM((W, count), BF16),
            pltpu.VMEM((3, W, count), BF16),
            pltpu.VMEM((W, count), F32),
            pltpu.VMEM((W, count), F32),
        ]
        + reduction_scratch(W, n, BF16) * 3,
        compiler_params=pltpu.CompilerParams(
            collective_id=0, has_side_effects=True, vmem_limit_bytes=56 * 1024 * 1024
        ),
        name="layer",
    )(lengths, tokens, cotangent, qkv, out, up, down, vec)


RATES = (RATE_MATRIX, RATE_OUTPUT, RATE_MATRIX, RATE_MATRIX)


def update_kernel(*refs):
    passed, sums, states = refs[0:2], refs[2:5], refs[5:17]
    passed_o, states_o = refs[17:19], refs[19:31]
    sums_v, ins, outs = refs[31:34], refs[34:46], refs[46:58]
    held = refs[58:60]
    pass_sem, sum_sem, in_sem, out_sem = refs[60:64]
    order = (3, 2, 0, 1)
    through_in = [pltpu.make_async_copy(passed[i], held[i], pass_sem.at[i]) for i in range(2)]
    through = [pltpu.make_async_copy(held[i], passed_o[i], pass_sem.at[2 + i]) for i in range(2)]
    sum_in = [pltpu.make_async_copy(sums[i], sums_v[i], sum_sem.at[i]) for i in range(3)]
    copy_in = [pltpu.make_async_copy(states[i], ins[i], in_sem.at[i]) for i in range(12)]
    copy_out = [pltpu.make_async_copy(outs[i], states_o[i], out_sem.at[i]) for i in range(12)]
    for copy in sum_in:
        copy.start()
    for w in order:
        for kind in range(3):
            copy_in[4 * kind + w].start()
    for copy in through_in:
        copy.start()
    for copy in sum_in:
        copy.wait()
    quarter = W // 4
    for w in order:
        if w == 2:
            for i in range(2):
                through_in[i].wait()
                through[i].start()
        for kind in range(3):
            copy_in[4 * kind + w].wait()
        rows, columns = ins[w].shape
        begin = (0, 3 * quarter, 0, 0)[w]
        group = sums_v[(2, 2, 1, 0)[w]]
        for j in range(columns // W):
            cut = slice(W * j, W * j + W)
            grad = group[begin + rows * j : begin + rows * j + rows].astype(F32)
            new = adamw(ins[w][:, cut], ins[4 + w][:, cut], ins[8 + w][:, cut], grad, RATES[w])
            for kind in range(3):
                outs[4 * kind + w][:, cut] = new[kind]
        for kind in range(3):
            copy_out[4 * kind + w].start()
    for copy in copy_out + through:
        copy.wait()


def update(activations, input_grad, sums, states):
    hbm = pl.BlockSpec(memory_space=pl.ANY)
    shapes = [jax.ShapeDtypeStruct(a.shape, a.dtype) for a in (activations, input_grad) + states]
    dma = pltpu.SemaphoreType.DMA
    return pl.pallas_call(
        update_kernel,
        out_shape=shapes,
        in_specs=[hbm] * 17,
        out_specs=[hbm] * 14,
        scratch_shapes=[pltpu.VMEM(a.shape, a.dtype) for a in sums + states + states + (activations, input_grad)]
        + [dma((4,)), dma((3,)), dma((12,)), dma((12,))],
        compiler_params=pltpu.CompilerParams(vmem_limit_bytes=56 * 1024 * 1024),
        name="update",
    )(activations, input_grad, *sums, *states)


def on_device(
    n,
    tokens,
    cotangent,
    lengths,
    qkv_weight,
    out_weight,
    up_weight,
    down_weight,
    vectors,
    qkv_first,
    out_first,
    up_first,
    down_first,
    vectors_first,
    qkv_second,
    out_second,
    up_second,
    down_second,
    vectors_second,
):
    share = vectors.shape[0]
    begin = lax.axis_index("zero") * share
    vec = lax.dynamic_update_slice(jnp.zeros((VROWS * 128,), F32), vectors, (begin,)).reshape(VROWS, 128)
    activations, input_grad, *sums, sum_vec = layer(
        n, lengths, tokens, cotangent, qkv_weight, out_weight, up_weight, down_weight, vec
    )
    vec_sum = lax.dynamic_slice(sum_vec.reshape(-1), (begin,), (share,))
    vec_new = adamw(vectors, vectors_first, vectors_second, vec_sum, RATE_VECTOR)
    states = (
        qkv_weight, out_weight, up_weight, down_weight,
        qkv_first, out_first, up_first, down_first,
        qkv_second, out_second, up_second, down_second,
    )
    news = update(activations, input_grad, tuple(sums), states)
    return (
        *news[0:6], vec_new[0], *news[6:10], vec_new[1], *news[10:14], vec_new[2],
    )


def solution(mesh):
    tokens = P(("dp", "zero"), None)
    params = (P("zero", None),) * 4 + (P("zero"),)
    return jax.shard_map(
        functools.partial(on_device, mesh.shape["dp"]),
        mesh=mesh,
        in_specs=(tokens,) * 3 + params * 3,
        out_specs=(tokens,) * 2 + params * 3,
        check_vma=False,
    )
```
